32 devices in a mesh: ctx: 4 (over y, x), head: 8 (over z, core).
Axes of the slice: x: 2, y: 2, z: 4, core: 2. Of those that a mesh axis runs over, the one named last changes fastest.
Arguments:
- queries: bfloat16 [2, 1024, 8192], P(None, 'ctx', 'head'), may hold values from -4.5 to 4.5
- key_rows: bfloat16 [2, 1024, 512], P(None, 'ctx'), may hold values from -4.5 to 4.5
- value_rows: bfloat16 [2, 1024, 512], P(None, 'ctx'), may hold values from -6 to 6
- out_weight: bfloat16 [8192, 8192], P('head'), may hold values from -0.0625 to 0.0625
- span_owner: int32 [2, 4], replicated, may hold values from 0 to 3, each once within a row
- vertical_blocks: int32 [64, 4], replicated, may hold values from 0 to 15, as said below
- slash_offsets: int32 [64, 4], replicated, may hold values from 1 to 15, as said below
Outputs:
- projected: bfloat16 [2, 1024, 8192], P(None, ('ctx', 'head'))
The draws below stay inside these ranges and needn't reach their ends.
Inputs may be any that keep to these rules, and one draw needn't show every extreme that they name: `vertical_blocks`: the 4 entries of a head are distinct block numbers. `slash_offsets`: the 4 entries of a head are distinct.
All inputs are finite; a program needn't handle non-finite values.
Results may differ from the reference program's by a relative error of at most 0.017.
Values may be sent and summed in bfloat16 or wider, within the bound.
A program may use at most 64 MiB of HBM per device.

```python
import math
import jax
import jax.numpy as jnp
from jax import lax

DW = 8192
QH = 64
KVH = 4
HD = 128
BLK = 128
SPAN = 256
STEPS = 2
NV = 4
NS = 4
SPANS = 4
ROWS = 1024
HEAD_GROUPS = 8
NB = 16


def draw_queries(key, part):
    full_shape = (STEPS, ROWS, QH * HD)
    entries = jnp.clip(jax.random.normal(jax.random.fold_in(key, 11), full_shape, jnp.float32), -4.5, 4.5)
    return entries.astype(jnp.bfloat16)


def draw_key_rows(key, part):
    full_shape = (STEPS, ROWS, KVH * HD)
    entries = jnp.clip(jax.random.normal(jax.random.fold_in(key, 12), full_shape, jnp.float32), -4.5, 4.5)
    return entries.astype(jnp.bfloat16)


def distinct_rows(key, lowest, highest, pick_count, row_total):

    def one_row(row_index):
        shuffled = lowest + jax.random.permutation(jax.random.fold_in(key, row_index), highest - lowest)
        return shuffled[:pick_count].astype(jnp.int32)
    shuffled_rows = jax.vmap(one_row)(jnp.arange(row_total))
    middle = lowest + 1 + jax.random.permutation(jax.random.fold_in(key, row_total + 7), highest - lowest - 2)
    first_row = jnp.concatenate([jnp.array([lowest, highest - 1], dtype=jnp.int32), middle[:pick_count - 2].astype(jnp.int32)])
    return shuffled_rows.at[0].set(first_row)


def draw_vertical_blocks(key, part):
    return distinct_rows(jax.random.fold_in(key, 21), 0, NB, NV, QH)


def draw_slash_offsets(key, part):
    return distinct_rows(jax.random.fold_in(key, 22), 1, NB, NS, QH)


def steps_of(own_key, shape, cuts, low, high):
    loudness = 1.0
    for position, parts in cuts:
        draws = jax.random.uniform(jax.random.fold_in(jax.random.fold_in(own_key, 6), position), (parts,), jnp.float32, low / len(cuts), high / len(cuts))
        loudness = loudness * jnp.repeat(jnp.exp(draws), shape[position] // parts).reshape((-1,) + (1,) * (len(shape) - 1 - position))
    return loudness


def gaussian(key, shape, scale, most, shards=(), kind=jnp.bfloat16):
    values = jax.random.normal(key, shape, jnp.float32) * scale
    if len(shards) > 0:
        values = steps_of(key, shape, shards, -0.22, 0.18) * values
    return jnp.clip(values, min=-most, max=most).astype(kind)


def setup_inputs(seed: int = 0) -> dict:
    seeds = jax.random.split(jax.random.key(seed), 8)
    queries = draw_queries(jax.random.fold_in(seeds[7], 71), 0)
    key_rows = draw_key_rows(jax.random.fold_in(seeds[7], 71), 0)
    value_rows = gaussian(seeds[2], (STEPS, ROWS, KVH * HD), 1.0, 6.0, ((1, 4),))
    out_weight = gaussian(seeds[3], (QH * HD, DW), (QH * HD) ** -0.5, 0.0625, ((0, 8),))
    span_owner = jax.vmap(lambda own: jax.random.permutation(own, SPANS))(jax.random.split(seeds[4], STEPS)).reshape((STEPS, SPANS)).astype(jnp.int32)
    vertical_blocks = draw_vertical_blocks(jax.random.fold_in(seeds[7], 71), 0)
    slash_offsets = draw_slash_offsets(jax.random.fold_in(seeds[7], 71), 0)
    return {"queries": queries, "key_rows": key_rows, "value_rows": value_rows, "out_weight": out_weight, "span_owner": span_owner, "vertical_blocks": vertical_blocks, "slash_offsets": slash_offsets}


def tile_blocks(block_ids, vertical, slanted, owner_flat, span_blocks, span_count):
    column = block_ids[:, None]
    vert_rows = jnp.broadcast_to(vertical[None, :], (block_ids.shape[0], vertical.shape[0]))
    slash_rows = column - slanted[None, :]
    vert_valid = vert_rows < column
    repeated = jnp.any(slash_rows[:, :, None] == vertical[None, None, :], axis=2)
    slash_valid = (slash_rows >= 0) & jnp.logical_not(repeated)
    chosen = jnp.concatenate([column, vert_rows, slash_rows], axis=1)
    allowed = jnp.concatenate([jnp.ones_like(column, dtype=bool), vert_valid, slash_valid], axis=1)
    chosen = jnp.where(allowed, chosen, column)
    span_index = chosen // span_blocks
    slot_ids = jnp.arange(owner_flat.shape[0], dtype=jnp.int32)
    holder = lax.optimization_barrier(jnp.sum(jnp.where(span_index[:, :, None] == slot_ids[None, None, :], owner_flat[None, None, :], 0), axis=2))
    step_index = span_index // span_count
    stored = (step_index * span_count + holder) * span_blocks + chosen % span_blocks
    return (stored.astype(jnp.int32), allowed)

def block_mask(allowed, block_rows):
    positions = jnp.arange(block_rows, dtype=jnp.int32)
    causal = positions[None, :] <= positions[:, None]
    tile_count = allowed.shape[1]
    first_tile = jnp.arange(tile_count, dtype=jnp.int32) == 0
    inside = causal[None, :, None, :] | jnp.logical_not(first_tile)[None, None, :, None]
    visible = allowed[:, None, :, None] & inside
    return visible.reshape(allowed.shape[0], block_rows, tile_count * block_rows)

def attend_head(query_tile_set, key_store, value_store, stored, allowed):
    block_count = stored.shape[0]
    tile_count = stored.shape[1]
    block_rows = query_tile_set.shape[1]
    head_features = query_tile_set.shape[2]
    key_tile_set = jnp.take(key_store, stored.reshape(-1), axis=0).reshape(block_count, tile_count * block_rows, head_features)
    value_tile_set = jnp.take(value_store, stored.reshape(-1), axis=0).reshape(block_count, tile_count * block_rows, head_features)
    logit_scores = jnp.einsum('zcs,zvs->zcv', query_tile_set.astype(jnp.float32), key_tile_set.astype(jnp.float32)) * (1.0 / math.sqrt(head_features))
    logit_scores = jnp.where(block_mask(allowed, block_rows), logit_scores, -jnp.inf)
    largest = lax.optimization_barrier(jnp.max(logit_scores, axis=2, keepdims=True))
    weights = jnp.exp(logit_scores - largest)
    totals = lax.optimization_barrier(jnp.sum(weights, axis=2, keepdims=True))
    rounded_values = lax.optimization_barrier(weights.astype(jnp.bfloat16))
    mixed_output = jnp.einsum('ynj,yjw->ynw', rounded_values.astype(jnp.float32), value_tile_set.astype(jnp.float32))
    return (mixed_output / totals).astype(jnp.bfloat16)

def reference(queries, key_rows, value_rows, out_weight, span_owner, vertical_blocks, slash_offsets):
    span_blocks = SPAN // BLK
    owners = span_owner.astype(jnp.int32)
    owner_flat = owners.reshape(-1)
    device_ids = jnp.arange(SPANS, dtype=jnp.int32)
    places = lax.optimization_barrier(jnp.sum(device_ids[None, None, :] * (owners[:, None, :] == device_ids[None, :, None]).astype(jnp.int32), axis=2)).astype(jnp.int32)
    step_ids = jnp.arange(STEPS, dtype=jnp.int32)[:, None, None]
    inner_ids = jnp.arange(span_blocks, dtype=jnp.int32)[None, None, :]
    block_ids = ((step_ids * SPANS + places[:, :, None]) * span_blocks + inner_ids).reshape(-1).astype(jnp.int32)
    group_size = QH // KVH

    def one_head(head_index):
        kv_head = head_index // group_size
        query_tile_set = lax.dynamic_slice_in_dim(queries, head_index * HD, HD, 2).reshape(-1, BLK, HD)
        key_store = lax.dynamic_slice_in_dim(key_rows, kv_head * HD, HD, 2).reshape(-1, BLK, HD)
        value_store = lax.dynamic_slice_in_dim(value_rows, kv_head * HD, HD, 2).reshape(-1, BLK, HD)
        vertical = lax.dynamic_index_in_dim(vertical_blocks, head_index, 0, keepdims=False).astype(jnp.int32)
        slanted = lax.dynamic_index_in_dim(slash_offsets, head_index, 0, keepdims=False).astype(jnp.int32)
        stored, allowed = tile_blocks(block_ids, vertical, slanted, owner_flat, span_blocks, SPANS)
        return attend_head(query_tile_set, key_store, value_store, stored, allowed).reshape(STEPS, ROWS, HD)
    heads_out = lax.map(one_head, jnp.arange(QH, dtype=jnp.int32))
    attended = jnp.transpose(heads_out, (1, 2, 0, 3)).reshape(STEPS * ROWS, QH * HD)
    group_width = QH * HD // HEAD_GROUPS

    def add_group(running, group_index):
        columns = lax.dynamic_slice_in_dim(attended, group_index * group_width, group_width, 1)
        weight_rows = lax.dynamic_slice_in_dim(out_weight, group_index * group_width, group_width, 0)
        partial_sum = jnp.dot(columns, weight_rows, preferred_element_type=jnp.float32)
        rounded_values = lax.optimization_barrier(partial_sum.astype(jnp.bfloat16))
        return (running + rounded_values.astype(jnp.float32), None)
    running = lax.scan(add_group, jnp.zeros((STEPS * ROWS, DW), jnp.float32), jnp.arange(HEAD_GROUPS, dtype=jnp.int32))[0]
    return running.astype(jnp.bfloat16).reshape(STEPS, ROWS, DW)
```

```python
import functools
import math

import jax
import jax.numpy as jnp
from jax import lax
from jax.experimental import pallas as pl
from jax.experimental.pallas import tpu as pltpu
from jax.sharding import PartitionSpec as P

QH = 64
KVH = 4
HD = 128
BLK = 128
STEPS = 2
NW = 1024
MESH = pl.DeviceIdType.MESH


def kernel(
    C, H, LH, RS, NV, NS,
    owner, vert, slant, q_hbm, k_hbm, v_hbm, w_hbm, out_hbm,
    q_ref, k0, k1, v0, v1, w_ref, att, part, crecv, urecv, drecv, obuf, tab_idx, tab_bias,
    load_sem, w_sem, own_sem, kv_send, kv_recv, fw_send, fw_recv,
    x_send, x_recv, z_send, u_recv, d_recv, o_sem, early_sem,
):
    Z = H // 2
    NC = w_ref.shape[0]
    SB = q_ref.shape[1] // BLK
    QR = 2 * RS
    NT = 1 + NV + NS
    c = lax.axis_index("ctx")
    h = lax.axis_index("head")
    z = h // 2
    j = h % 2
    sib = z * 2 + 1 - j
    kbufs, vbufs = (k0, k1), (v0, v1)

    kv_head = (h * LH) // (QH // KVH)
    cols = pl.ds(pl.multiple_of(kv_head * HD, HD), HD)
    own_rows = pl.ds(pl.multiple_of(j * BLK, BLK), BLK)

    own_copies = []
    for s in range(STEPS):
        for t, (src, bufs) in enumerate(((k_hbm, kbufs), (v_hbm, vbufs))):
            for b in range(SB):
                cp = pltpu.make_async_copy(
                    src.at[s, pl.ds(b * BLK, BLK), cols], bufs[s].at[s * C * SB + SB * c + b], own_sem.at[s, t, b]
                )
                cp.start()
                own_copies.append((s, cp))
    q_copy = pltpu.make_async_copy(q_hbm, q_ref, load_sem)
    q_copy.start()

    def w_copy(n):
        return pltpu.make_async_copy(
            w_hbm.at[:, pl.ds(pl.multiple_of(n * NW, NW), NW)], w_ref.at[n], w_sem.at[n]
        )

    barrier = pltpu.get_barrier_semaphore()
    pl.semaphore_signal(barrier, inc=1, device_id={"head": sib}, device_id_type=MESH)

    @pl.when(z > 0)
    def _():
        pl.semaphore_signal(barrier, inc=1, device_id={"head": h - 2}, device_id_type=MESH)

    @pl.when(z < Z - 1)
    def _():
        pl.semaphore_signal(barrier, inc=1, device_id={"head": h + 2}, device_id_type=MESH)

    for p in range(1, C):
        pl.semaphore_signal(barrier, inc=1, device_id={"ctx": lax.rem(c + p, C)}, device_id_type=MESH)
    pl.semaphore_wait(barrier, C + (z > 0).astype(jnp.int32) + (z < Z - 1).astype(jnp.int32))

    def kv_copy(s, t, p):
        src = (k_hbm, v_hbm)[t]
        buf = (kbufs, vbufs)[t][s]
        return pltpu.make_async_remote_copy(
            src_ref=src.at[s, own_rows, cols],
            dst_ref=buf.at[s * C * SB + SB * c + j],
            send_sem=kv_send.at[s, t, p],
            recv_sem=kv_recv.at[s, t, c],
            device_id={"ctx": lax.rem(c + p, C)},
            device_id_type=MESH,
        )

    def kv_arrival(s, t, origin, block, sem):
        buf = (kbufs, vbufs)[t][s]
        dst = buf.at[s * C * SB + SB * origin + block]
        return pltpu.make_async_copy(dst, dst, sem.at[s, t, origin])

    def fw_copy(s, t, p):
        origin = lax.rem(c + C - p, C)
        buf = (kbufs, vbufs)[t][s]
        return pltpu.make_async_remote_copy(
            src_ref=buf.at[s * C * SB + SB * origin + j],
            dst_ref=buf.at[s * C * SB + SB * origin + j],
            send_sem=fw_send.at[s, t, p],
            recv_sem=fw_recv.at[s, t, origin],
            device_id={"head": sib},
            device_id_type=MESH,
        )

    for s in range(STEPS):
        for p in range(1, C):
            for t in range(2):
                kv_copy(s, t, p).start()
    for n in range(NC):
        w_copy(n).start()

    for s in range(STEPS):
        place = jnp.int32(0)
        for p in range(C):
            place = jnp.where(owner[s, p] == c, p, place)

        def fill(i, carry, s=s, place=place):
            b = i // LH
            lh = i % LH
            head = h * LH + lh
            block = (s * C + place) * SB + b

            def put(tile, chosen, allowed):
                chosen = jnp.where(allowed, chosen, block)
                span = chosen // SB
                step = span // C
                holder = owner[step, span - step * C]
                tab_idx[s, i, tile] = (step * C + holder) * SB + chosen - span * SB
                tab_bias[s, i, tile] = jnp.where(allowed, 0.0, -1e30).astype(jnp.float32)

            vs = [vert[head, a] for a in range(NV)]
            put(0, block, block == block)
            for a in range(NV):
                put(1 + a, vs[a], vs[a] < block)
            for a in range(NS):
                row = block - slant[head, a]
                ok = row >= 0
                for x in vs:
                    ok = jnp.logical_and(ok, row != x)
                put(1 + NV + a, row, ok)
            return carry

        lax.fori_loop(0, SB * LH, fill, 0)

    scale = math.log2(math.e) / math.sqrt(HD)

    def attend(d, s):
        r0 = pl.multiple_of(d * QR, QR)
        b = r0 // BLK
        within = r0 - b * BLK
        row_ids = lax.broadcasted_iota(jnp.int32, (QR, BLK), 0) + within
        col_ids = lax.broadcasted_iota(jnp.int32, (QR, BLK), 1)
        causal = col_ids <= row_ids

        def one(lh):
            hc = pl.ds(pl.multiple_of(lh * HD, HD), HD)
            i = b * LH + lh
            qt = q_ref[s, pl.ds(r0, QR), hc]
            ids = [tab_idx[s, i, t] for t in range(NT)]

            def tile(bufs, t):
                return bufs[s][ids[t]]

            kt = jnp.concatenate([tile(kbufs, t) for t in range(NT)], axis=0)
            sc = lax.dot_general(qt, kt, (((1,), (1,)), ((), ())), preferred_element_type=jnp.float32)
            pieces = []
            for t in range(NT):
                x = sc[:, t * BLK:(t + 1) * BLK] * scale
                if t == 0:
                    x = jnp.where(causal, x, -1e30)
                else:
                    x = x + tab_bias[s, i, t]
                pieces.append(x)
            top = pieces[0]
            for x in pieces[1:]:
                top = jnp.maximum(top, x)
            top = jnp.max(top, axis=1, keepdims=True)
            ws = [jnp.exp2(x - top) for x in pieces]
            tot = ws[0]
            for x in ws[1:]:
                tot = tot + x
            tot = jnp.sum(tot, axis=1, keepdims=True)
            wt = jnp.concatenate([x.astype(jnp.bfloat16) for x in ws], axis=1)
            vt = jnp.concatenate([tile(vbufs, t) for t in range(NT)], axis=0)
            mixed = jnp.dot(wt, vt, preferred_element_type=jnp.float32) / tot
            mixed = mixed.astype(jnp.bfloat16)
            att[pl.ds(s * RS, RS), hc] = mixed[:RS]
            att[pl.ds((STEPS + s) * RS, RS), hc] = mixed[RS:]

        def body(i, carry):
            one(2 * i)
            one(2 * i + 1)
            return carry

        lax.fori_loop(0, LH // 2, body, 0)

    def x_copy(d, n):
        return pltpu.make_async_remote_copy(
            src_ref=part.at[d, n, 1 - j], dst_ref=crecv.at[d, n],
            send_sem=x_send.at[d, n], recv_sem=x_recv.at[d, n],
            device_id={"head": sib}, device_id_type=MESH,
        )

    def u_copy(d, n):
        return pltpu.make_async_remote_copy(
            src_ref=part.at[d, n, j], dst_ref=urecv.at[d, n],
            send_sem=z_send.at[d, n], recv_sem=u_recv.at[d, n],
            device_id={"head": h + 2}, device_id_type=MESH,
        )

    def d_copy(d, n):
        return pltpu.make_async_remote_copy(
            src_ref=part.at[d, n, j], dst_ref=drecv.at[d, n],
            send_sem=z_send.at[d, n], recv_sem=d_recv.at[d, n],
            device_id={"head": h - 2}, device_id_type=MESH,
        )

    f32 = jnp.float32

    def process(d, n):
        x_copy(d, n).wait_recv()

        @pl.when(d > z)
        def _():
            @pl.when(z > 0)
            def _():
                u_copy(d, n).wait_recv()
                part[d, n, j] = (
                    part[d, n, j].astype(f32) + crecv[d, n].astype(f32) + urecv[d, n].astype(f32)
                ).astype(jnp.bfloat16)

            @pl.when(z == 0)
            def _():
                part[d, n, j] = (part[d, n, j].astype(f32) + crecv[d, n].astype(f32)).astype(jnp.bfloat16)

            u_copy(d, n).start()

        @pl.when(d < z)
        def _():
            @pl.when(z < Z - 1)
            def _():
                d_copy(d, n).wait_recv()
                part[d, n, j] = (
                    part[d, n, j].astype(f32) + crecv[d, n].astype(f32) + drecv[d, n].astype(f32)
                ).astype(jnp.bfloat16)

            @pl.when(z == Z - 1)
            def _():
                part[d, n, j] = (part[d, n, j].astype(f32) + crecv[d, n].astype(f32)).astype(jnp.bfloat16)

            d_copy(d, n).start()

    low = z < Z // 2
    zm = jnp.where(low, z, Z - 1 - z)

    def dest_of(t):
        paired = jnp.where(t % 2 == 0, Z - 1 - t // 2, t // 2)
        d = jnp.where(t < 2 * zm, paired, Z - 1 - (t - zm))
        return jnp.where(low, d, Z - 1 - d)

    at_end = jnp.logical_or(z == 0, z == Z - 1)

    def project(t, d, first):
        prev = dest_of(jnp.maximum(t - 1, 0))

        def step(n, carry):
            if first:
                w_copy(n).wait()
            y = jnp.dot(att[...], w_ref[n], preferred_element_type=f32).astype(jnp.bfloat16)
            part[d, n, 0] = y[: STEPS * RS]
            part[d, n, 1] = y[STEPS * RS:]
            x_copy(d, n).start()

            @pl.when(jnp.logical_and(at_end, jnp.logical_and(n > 0, d != z)))
            def _():
                process(d, n - 1)

            if not first:
                @pl.when(jnp.logical_not(at_end))
                def _():
                    process(prev, n)
            return carry

        lax.fori_loop(0, NC, step, 0)

        @pl.when(jnp.logical_and(at_end, d != z))
        def _():
            process(d, NC - 1)

    early = [
        pltpu.make_async_copy(bufs[0], bufs[1].at[pl.ds(0, C * SB)], early_sem.at[t])
        for t, bufs in enumerate((kbufs, vbufs))
    ]
    q_copy.wait()
    d_first = dest_of(jnp.int32(0))
    for s in range(STEPS):
        for p in range(1, C):
            origin = lax.rem(c + C - p, C)
            for t in range(2):
                kv_arrival(s, t, origin, j, kv_recv).wait()
                fw_copy(s, t, p).start()
        for step_of, cp in own_copies:
            if step_of == s:
                cp.wait()
        for p in range(1, C):
            origin = lax.rem(c + C - p, C)
            for t in range(2):
                kv_arrival(s, t, origin, 1 - j, fw_recv).wait()
        if s == 0:
            for cp in early:
                cp.start()
        else:
            for cp in early:
                cp.wait()
        attend(d_first, s)
    project(jnp.int32(0), d_first, True)

    def rest(t, carry):
        d = dest_of(t)
        for s in range(STEPS):
            attend(d, s)
        project(t, d, False)
        return carry

    lax.fori_loop(1, Z, rest, 0)

    def o_copy(n, s):
        return pltpu.make_async_copy(
            obuf.at[n, pl.ds(s * RS, RS)],
            out_hbm.at[s, :, pl.ds(pl.multiple_of(n * NW, NW), NW)],
            o_sem.at[n, s],
        )

    def finish(n, carry):
        x_copy(z, n).wait_recv()

        @pl.when(z == 0)
        def _():
            d_copy(z, n).wait_recv()
            obuf[n] = (
                part[z, n, j].astype(f32) + crecv[z, n].astype(f32) + drecv[z, n].astype(f32)
            ).astype(jnp.bfloat16)

        @pl.when(z == Z - 1)
        def _():
            u_copy(z, n).wait_recv()
            obuf[n] = (
                part[z, n, j].astype(f32) + crecv[z, n].astype(f32) + urecv[z, n].astype(f32)
            ).astype(jnp.bfloat16)

        @pl.when(jnp.logical_not(at_end))
        def _():
            d_copy(z, n).wait_recv()
            u_copy(z, n).wait_recv()
            obuf[n] = (
                part[z, n, j].astype(f32) + crecv[z, n].astype(f32)
                + drecv[z, n].astype(f32) + urecv[z, n].astype(f32)
            ).astype(jnp.bfloat16)

        for s in range(STEPS):
            o_copy(n, s).start()
        return carry

    lax.fori_loop(0, NC, finish, 0)

    for s in range(STEPS):
        for p in range(1, C):
            for t in range(2):
                kv_copy(s, t, p).wait_send()
                fw_copy(s, t, p).wait_send()

    def drain(i, carry):
        d = i // NC
        n = i % NC
        x_copy(d, n).wait_send()

        @pl.when(d > z)
        def _():
            u_copy(d, n).wait_send()

        @pl.when(d < z)
        def _():
            d_copy(d, n).wait_send()

        return carry

    lax.fori_loop(0, Z * NC, drain, 0)

    def drain_out(n, carry):
        for s in range(STEPS):
            o_copy(n, s).wait()
        return carry

    lax.fori_loop(0, NC, drain_out, 0)


def solution(mesh):
    C = mesh.shape["ctx"]
    H = mesh.shape["head"]
    Z = H // 2

    def local(queries, key_rows, value_rows, out_weight, span_owner, vertical_blocks, slash_offsets):
        steps, span_rows, width = queries.shape
        depth, DW = out_weight.shape
        LH = width // HD
        RS = span_rows // H
        SB = span_rows // BLK
        NC = DW // NW
        NV, NS = vertical_blocks.shape[1], slash_offsets.shape[1]
        NT = 1 + NV + NS
        bf = jnp.bfloat16
        kv0 = pltpu.VMEM((C * SB, BLK, HD), bf)
        kv1 = pltpu.VMEM((STEPS * C * SB, BLK, HD), bf)
        dma = pltpu.SemaphoreType.DMA
        smem = pl.BlockSpec(memory_space=pltpu.SMEM)
        anyspec = pl.BlockSpec(memory_space=pl.ANY)
        MR = STEPS * RS
        return pl.pallas_call(
            functools.partial(kernel, C, H, LH, RS, NV, NS),
            out_shape=jax.ShapeDtypeStruct((STEPS, RS, DW), bf),
            in_specs=[smem] * 3 + [anyspec] * 4,
            out_specs=anyspec,
            scratch_shapes=[
                pltpu.VMEM((STEPS, span_rows, width), bf),
                kv0, kv1, kv0, kv1,
                pltpu.VMEM((NC, depth, NW), bf),
                pltpu.VMEM((2 * MR, width), bf),
                pltpu.VMEM((Z, NC, 2, MR, NW), bf),
                pltpu.VMEM((Z, NC, MR, NW), bf),
                pltpu.VMEM((Z, NC, MR, NW), bf),
                pltpu.VMEM((Z, NC, MR, NW), bf),
                pltpu.VMEM((NC, MR, NW), bf),
                pltpu.SMEM((STEPS, SB * LH, NT), jnp.int32),
                pltpu.SMEM((STEPS, SB * LH, NT), jnp.float32),
                dma, dma((NC,)), dma((STEPS, 2, SB)),
                dma((STEPS, 2, C)), dma((STEPS, 2, C)), dma((STEPS, 2, C)), dma((STEPS, 2, C)),
                dma((Z, NC)), dma((Z, NC)), dma((Z, NC)), dma((Z, NC)), dma((Z, NC)),
                dma((NC, STEPS)), dma((2,)),
            ],
            compiler_params=pltpu.CompilerParams(
                collective_id=0, has_side_effects=True, vmem_limit_bytes=58 * 1024 * 1024
            ),
            cost_estimate=pl.CostEstimate(
                flops=2 * STEPS * span_rows * depth * DW, bytes_accessed=depth * DW * 2, transcendentals=0
            ),
        )(span_owner, vertical_blocks, slash_offsets, queries, key_rows, value_rows, out_weight)

    in_specs = (
        P(None, "ctx", "head"),
        P(None, "ctx", None),
        P(None, "ctx", None),
        P("head", None),
        P(),
        P(),
        P(),
    )
    return jax.shard_map(
        local, mesh=mesh, in_specs=in_specs, out_specs=P(None, ("ctx", "head"), None), check_vma=False
    )
```

```python
import functools
import math

import jax
import jax.numpy as jnp
from jax import lax
from jax.experimental import pallas as pl
from jax.experimental.pallas import tpu as pltpu
from jax.sharding import PartitionSpec as P

QH = 64
KVH = 4
HD = 128
BLK = 128
STEPS = 2
NW = 1024
MESH = pl.DeviceIdType.MESH


def kernel(
    C, H, LH, RS, NV, NS,
    owner, vert, slant, q_hbm, k_hbm, v_hbm, w_hbm, out_hbm,
    q_ref, k0, k1, v0, v1, w_ref, att, part, crecv, urecv, drecv, obuf, tab_idx, tab_bias,
    load_sem, w_sem, own_sem, kv_send, kv_recv, fw_send, fw_recv,
    x_send, x_recv, z_send, u_recv, d_recv, o_sem, early_sem,
):
    Z = H // 2
    NC = w_ref.shape[0]
    SB = q_ref.shape[1] // BLK
    QR = 2 * RS
    NT = 1 + NV + NS
    c = lax.axis_index("ctx")
    h = lax.axis_index("head")
    z = h // 2
    j = h % 2
    sib = z * 2 + 1 - j
    kbufs, vbufs = (k0, k1), (v0, v1)

    kv_head = (h * LH) // (QH // KVH)
    cols = pl.ds(pl.multiple_of(kv_head * HD, HD), HD)
    own_rows = pl.ds(pl.multiple_of(j * BLK, BLK), BLK)

    own_copies = []
    for s in range(STEPS):
        for t, (src, bufs) in enumerate(((k_hbm, kbufs), (v_hbm, vbufs))):
            for b in range(SB):
                cp = pltpu.make_async_copy(
                    src.at[s, pl.ds(b * BLK, BLK), cols], bufs[s].at[s * C * SB + SB * c + b], own_sem.at[s, t, b]
                )
                cp.start()
                own_copies.append((s, cp))
    q_copy = pltpu.make_async_copy(q_hbm, q_ref, load_sem)
    q_copy.start()

    def w_copy(n):
        return pltpu.make_async_copy(
            w_hbm.at[:, pl.ds(pl.multiple_of(n * NW, NW), NW)], w_ref.at[n], w_sem.at[n]
        )

    for n in range(NC):
        w_copy(n).start()

    barrier = pltpu.get_barrier_semaphore()
    pl.semaphore_signal(barrier, inc=1, device_id={"head": sib}, device_id_type=MESH)

    @pl.when(z > 0)
    def _():
        pl.semaphore_signal(barrier, inc=1, device_id={"head": h - 2}, device_id_type=MESH)

    @pl.when(z < Z - 1)
    def _():
        pl.semaphore_signal(barrier, inc=1, device_id={"head": h + 2}, device_id_type=MESH)

    for p in range(1, C):
        pl.semaphore_signal(barrier, inc=1, device_id={"ctx": lax.rem(c + p, C)}, device_id_type=MESH)
    pl.semaphore_wait(barrier, C + (z > 0).astype(jnp.int32) + (z < Z - 1).astype(jnp.int32))

    def kv_copy(s, t, p):
        src = (k_hbm, v_hbm)[t]
        buf = (kbufs, vbufs)[t][s]
        return pltpu.make_async_remote_copy(
            src_ref=src.at[s, own_rows, cols],
            dst_ref=buf.at[s * C * SB + SB * c + j],
            send_sem=kv_send.at[s, t, p],
            recv_sem=kv_recv.at[s, t, c],
            device_id={"ctx": lax.rem(c + p, C)},
            device_id_type=MESH,
        )

    def kv_arrival(s, t, origin, block, sem):
        buf = (kbufs, vbufs)[t][s]
        dst = buf.at[s * C * SB + SB * origin + block]
        return pltpu.make_async_copy(dst, dst, sem.at[s, t, origin])

    def fw_copy(s, t, p):
        origin = lax.rem(c + C - p, C)
        buf = (kbufs, vbufs)[t][s]
        return pltpu.make_async_remote_copy(
            src_ref=buf.at[s * C * SB + SB * origin + j],
            dst_ref=buf.at[s * C * SB + SB * origin + j],
            send_sem=fw_send.at[s, t, p],
            recv_sem=fw_recv.at[s, t, origin],
            device_id={"head": sib},
            device_id_type=MESH,
        )

    for s in range(STEPS):
        for p in range(1, C):
            for t in range(2):
                kv_copy(s, t, p).start()
    low = z < Z // 2
    zm = jnp.where(low, z, Z - 1 - z)

    def dest_of(t):
        paired = jnp.where(t % 2 == 0, Z - 1 - t // 2, t // 2)
        d = jnp.where(t < 2 * zm, paired, Z - 1 - (t - zm))
        return jnp.where(low, d, Z - 1 - d)

    d_first = dest_of(jnp.int32(0))
    b_first = (d_first * QR) // BLK

    def fill(s, b):
        place = jnp.int32(0)
        for p in range(C):
            place = jnp.where(owner[s, p] == c, p, place)
        block = (s * C + place) * SB + b

        def one_head(lh, carry):
            i = b * LH + lh
            head = h * LH + lh

            def put(tile, chosen, allowed):
                chosen = jnp.where(allowed, chosen, block)
                span = chosen // SB
                step = span // C
                holder = owner[step, span - step * C]
                tab_idx[s, i, tile] = (step * C + holder) * SB + chosen - span * SB
                tab_bias[s, i, tile] = jnp.where(allowed, 0.0, -1e30).astype(jnp.float32)

            vs = [vert[a, head] for a in range(NV)]
            put(0, block, block == block)
            for a in range(NV):
                put(1 + a, vs[a], vs[a] < block)
            for a in range(NS):
                row = block - slant[a, head]
                ok = row >= 0
                for x in vs:
                    ok = jnp.logical_and(ok, row != x)
                put(1 + NV + a, row, ok)
            return carry

        lax.fori_loop(0, LH, one_head, 0)

    for s in range(STEPS):
        fill(s, b_first)

    scale = math.log2(math.e) / math.sqrt(HD)

    def attend(d, s):
        r0 = pl.multiple_of(d * QR, QR)
        b = r0 // BLK
        within = r0 - b * BLK
        row_ids = lax.broadcasted_iota(jnp.int32, (QR, BLK), 0) + within
        col_ids = lax.broadcasted_iota(jnp.int32, (QR, BLK), 1)
        causal = col_ids <= row_ids

        def one(lh):
            hc = pl.ds(pl.multiple_of(lh * HD, HD), HD)
            i = b * LH + lh
            qt = q_ref[s, pl.ds(r0, QR), hc]
            ids = [tab_idx[s, i, t] for t in range(NT)]

            def tile(bufs, t):
                return bufs[s][ids[t]]

            kt = jnp.concatenate([tile(kbufs, t) for t in range(NT)], axis=0)
            sc = lax.dot_general(qt, kt, (((1,), (1,)), ((), ())), preferred_element_type=jnp.float32)
            pieces = []
            for t in range(NT):
                x = sc[:, t * BLK:(t + 1) * BLK] * scale
                if t == 0:
                    x = jnp.where(causal, x, -1e30)
                else:
                    x = x + tab_bias[s, i, t]
                pieces.append(x)
            top = pieces[0]
            for x in pieces[1:]:
                top = jnp.maximum(top, x)
            top = jnp.max(top, axis=1, keepdims=True)
            ws = [jnp.exp2(x - top) for x in pieces]
            tot = ws[0]
            for x in ws[1:]:
                tot = tot + x
            tot = jnp.sum(tot, axis=1, keepdims=True)
            wt = jnp.concatenate([x.astype(jnp.bfloat16) for x in ws], axis=1)
            vt = jnp.concatenate([tile(vbufs, t) for t in range(NT)], axis=0)
            mixed = jnp.dot(wt, vt, preferred_element_type=jnp.float32) / tot
            mixed = mixed.astype(jnp.bfloat16)
            att[pl.ds(s * QR, QR), hc] = mixed

        def body(i, carry):
            one(2 * i)
            one(2 * i + 1)
            return carry

        lax.fori_loop(0, LH // 2, body, 0)

    def x_copy(d, n, s):
        return pltpu.make_async_remote_copy(
            src_ref=part.at[d, n, s, 1 - j], dst_ref=crecv.at[d, n, s],
            send_sem=x_send.at[d, n, s], recv_sem=x_recv.at[d, n, s],
            device_id={"head": sib}, device_id_type=MESH,
        )

    def u_copy(d, n, s):
        return pltpu.make_async_remote_copy(
            src_ref=part.at[d, n, s, j], dst_ref=urecv.at[d, n, s],
            send_sem=z_send.at[d, n, s], recv_sem=u_recv.at[d, n, s],
            device_id={"head": h + 2}, device_id_type=MESH,
        )

    def d_copy(d, n, s):
        return pltpu.make_async_remote_copy(
            src_ref=part.at[d, n, s, j], dst_ref=drecv.at[d, n, s],
            send_sem=z_send.at[d, n, s], recv_sem=d_recv.at[d, n, s],
            device_id={"head": h - 2}, device_id_type=MESH,
        )

    f32 = jnp.float32

    def process(d, n, s):
        x_copy(d, n, s).wait_recv()

        def ready(*more):
            total = part[d, n, s, j].astype(f32) + crecv[d, n, s].astype(f32)
            for buf in more:
                total = total + buf[d, n, s].astype(f32)
            part[d, n, s, j] = total.astype(jnp.bfloat16)

        @pl.when(d > z)
        def _():
            @pl.when(z > 0)
            def _():
                u_copy(d, n, s).wait_recv()
                ready(urecv)

            @pl.when(z == 0)
            def _():
                ready()

            u_copy(d, n, s).start()

        @pl.when(d < z)
        def _():
            @pl.when(z < Z - 1)
            def _():
                d_copy(d, n, s).wait_recv()
                ready(drecv)

            @pl.when(z == Z - 1)
            def _():
                ready()

            d_copy(d, n, s).start()

    at_end = jnp.logical_or(z == 0, z == Z - 1)

    def send_parts(d, n, y, ss):
        for i, s in enumerate(ss):
            for jj in range(2):
                part[d, n, s, jj] = y[(2 * i + jj) * RS:(2 * i + jj + 1) * RS]
            x_copy(d, n, s).start()

    def project_first(d, s):
        def step(n, carry):
            if s == 0:
                w_copy(n).wait()
            y = jnp.dot(att[pl.ds(s * QR, QR)], w_ref[n], preferred_element_type=f32)
            send_parts(d, n, y.astype(jnp.bfloat16), (s,))

            @pl.when(jnp.logical_and(at_end, n > 0))
            def _():
                process(d, n - 1, s)

            return carry

        lax.fori_loop(0, NC, step, 0)

        @pl.when(at_end)
        def _():
            process(d, NC - 1, s)

    def project(t, d):
        prev = dest_of(t - 1)

        def step(n, carry):
            y = jnp.dot(att[...], w_ref[n], preferred_element_type=f32)
            send_parts(d, n, y.astype(jnp.bfloat16), range(STEPS))

            @pl.when(jnp.logical_and(at_end, jnp.logical_and(n > 0, d != z)))
            def _():
                for s in range(STEPS):
                    process(d, n - 1, s)

            @pl.when(jnp.logical_not(at_end))
            def _():
                for s in range(STEPS):
                    process(prev, n, s)

            return carry

        lax.fori_loop(0, NC, step, 0)

        @pl.when(jnp.logical_and(at_end, d != z))
        def _():
            for s in range(STEPS):
                process(d, NC - 1, s)

    early = [
        pltpu.make_async_copy(bufs[0], bufs[1].at[pl.ds(0, C * SB)], early_sem.at[t])
        for t, bufs in enumerate((kbufs, vbufs))
    ]
    q_copy.wait()
    for s in range(STEPS):
        for p in range(1, C):
            origin = lax.rem(c + C - p, C)
            for t in range(2):
                kv_arrival(s, t, origin, j, kv_recv).wait()
                fw_copy(s, t, p).start()
        for step_of, cp in own_copies:
            if step_of == s:
                cp.wait()
        for p in range(1, C):
            origin = lax.rem(c + C - p, C)
            for t in range(2):
                kv_arrival(s, t, origin, 1 - j, fw_recv).wait()
        if s == 0:
            for cp in early:
                cp.start()
        else:
            for cp in early:
                cp.wait()
        attend(d_first, s)
        project_first(d_first, s)
    for k in range(1, SB):
        for s in range(STEPS):
            fill(s, lax.rem(b_first + k, SB))

    def rest(t, carry):
        d = dest_of(t)
        for s in range(STEPS):
            attend(d, s)
        project(t, d)
        return carry

    lax.fori_loop(1, Z, rest, 0)

    def o_copy(n, s):
        return pltpu.make_async_copy(
            obuf.at[n, s],
            out_hbm.at[s, :, pl.ds(pl.multiple_of(n * NW, NW), NW)],
            o_sem.at[n, s],
        )

    def finish(n, carry):
        for s in range(STEPS):
            def done(*more, s=s):
                total = part[z, n, s, j].astype(f32) + crecv[z, n, s].astype(f32)
                for buf in more:
                    total = total + buf[z, n, s].astype(f32)
                obuf[n, s] = total.astype(jnp.bfloat16)

            x_copy(z, n, s).wait_recv()

            @pl.when(z == 0)
            def _():
                d_copy(z, n, s).wait_recv()
                done(drecv)

            @pl.when(z == Z - 1)
            def _():
                u_copy(z, n, s).wait_recv()
                done(urecv)

            @pl.when(jnp.logical_not(at_end))
            def _():
                d_copy(z, n, s).wait_recv()
                u_copy(z, n, s).wait_recv()
                done(drecv, urecv)

            o_copy(n, s).start()
        return carry

    def drain_z(i, carry):
        d = i // NC
        n = i % NC

        @pl.when(d > z)
        def _():
            for s in range(STEPS):
                u_copy(d, n, s).wait_send()

        @pl.when(d < z)
        def _():
            for s in range(STEPS):
                d_copy(d, n, s).wait_send()

        return carry

    def drain_x(i, carry):
        for s in range(STEPS):
            x_copy(i // NC, i % NC, s).wait_send()
        return carry

    for s in range(STEPS):
        for p in range(1, C):
            for t in range(2):
                kv_copy(s, t, p).wait_send()
                fw_copy(s, t, p).wait_send()
    lax.fori_loop(0, Z * NC, drain_x, 0)

    @pl.when(jnp.logical_not(at_end))
    def _():
        lax.fori_loop(0, Z * NC, drain_z, 0)

    lax.fori_loop(0, NC, finish, 0)

    @pl.when(at_end)
    def _():
        lax.fori_loop(0, Z * NC, drain_z, 0)

    def drain_out(n, carry):
        for s in range(STEPS):
            o_copy(n, s).wait()
        return carry

    lax.fori_loop(0, NC, drain_out, 0)


def solution(mesh):
    C = mesh.shape["ctx"]
    H = mesh.shape["head"]
    Z = H // 2

    def local(queries, key_rows, value_rows, out_weight, span_owner, vertical_blocks, slash_offsets):
        steps, span_rows, width = queries.shape
        depth, DW = out_weight.shape
        LH = width // HD
        RS = span_rows // H
        SB = span_rows // BLK
        NC = DW // NW
        NV, NS = vertical_blocks.shape[1], slash_offsets.shape[1]
        NT = 1 + NV + NS
        bf = jnp.bfloat16
        kv0 = pltpu.VMEM((C * SB, BLK, HD), bf)
        kv1 = pltpu.VMEM((STEPS * C * SB, BLK, HD), bf)
        dma = pltpu.SemaphoreType.DMA
        smem = pl.BlockSpec(memory_space=pltpu.SMEM)
        anyspec = pl.BlockSpec(memory_space=pl.ANY)
        MR = STEPS * RS
        return pl.pallas_call(
            functools.partial(kernel, C, H, LH, RS, NV, NS),
            out_shape=jax.ShapeDtypeStruct((STEPS, RS, DW), bf),
            in_specs=[smem] * 3 + [anyspec] * 4,
            out_specs=anyspec,
            scratch_shapes=[
                pltpu.VMEM((STEPS, span_rows, width), bf),
                kv0, kv1, kv0, kv1,
                pltpu.VMEM((NC, depth, NW), bf),
                pltpu.VMEM((2 * MR, width), bf),
                pltpu.VMEM((Z, NC, STEPS, 2, RS, NW), bf),
                pltpu.VMEM((Z, NC, STEPS, RS, NW), bf),
                pltpu.VMEM((Z, NC, STEPS, RS, NW), bf),
                pltpu.VMEM((Z, NC, STEPS, RS, NW), bf),
                pltpu.VMEM((NC, STEPS, RS, NW), bf),
                pltpu.SMEM((STEPS, SB * LH, NT), jnp.int32),
                pltpu.SMEM((STEPS, SB * LH, NT), jnp.float32),
                dma, dma((NC,)), dma((STEPS, 2, SB)),
                dma((STEPS, 2, C)), dma((STEPS, 2, C)), dma((STEPS, 2, C)), dma((STEPS, 2, C)),
                *[dma((Z, NC, STEPS))] * 5,
                dma((NC, STEPS)), dma((2,)),
            ],
            compiler_params=pltpu.CompilerParams(
                collective_id=0, has_side_effects=True, vmem_limit_bytes=58 * 1024 * 1024
            ),
            cost_estimate=pl.CostEstimate(
                flops=2 * STEPS * span_rows * depth * DW, bytes_accessed=depth * DW * 2, transcendentals=0
            ),
        )(span_owner, vertical_blocks.T, slash_offsets.T, queries, key_rows, value_rows, out_weight)

    in_specs = (
        P(None, "ctx", "head"),
        P(None, "ctx", None),
        P(None, "ctx", None),
        P("head", None),
        P(),
        P(),
        P(),
    )
    return jax.shard_map(
        local, mesh=mesh, in_specs=in_specs, out_specs=P(None, ("ctx", "head"), None), check_vma=False
    )
```

```python
import functools
import math

import jax
import jax.numpy as jnp
from jax import lax
from jax.experimental import pallas as pl
from jax.experimental.pallas import tpu as pltpu
from jax.sharding import PartitionSpec as P

QH = 64
KVH = 4
HD = 128
BLK = 128
STEPS = 2
NW = 1024
MESH = pl.DeviceIdType.MESH


def kernel(
    C, H, LH, RS, NV, NS,
    owner, vert, slant, q_hbm, k_hbm, v_hbm, w_hbm, out_hbm,
    q_ref, k0, k1, v0, v1, kt_ref, w_ref, att, part, crecv, urecv, drecv, obuf, tab_idx, tab_bias,
    load_sem, w_sem, own_sem, kv_send, kv_recv, fw_send, fw_recv,
    x_send, x_recv, z_send, u_recv, d_recv, o_sem, early_sem,
):
    Z = H // 2
    NC = w_ref.shape[0]
    SB = q_ref.shape[1] // BLK
    QR = 2 * RS
    NT = 1 + NV + NS
    c = lax.axis_index("ctx")
    h = lax.axis_index("head")
    z = h // 2
    j = h % 2
    sib = z * 2 + 1 - j
    kbufs, vbufs = (k0, k1), (v0, v1)

    kv_head = (h * LH) // (QH // KVH)
    cols = pl.ds(pl.multiple_of(kv_head * HD, HD), HD)
    own_rows = pl.ds(pl.multiple_of(j * BLK, BLK), BLK)

    def base(s, t):
        return s * C * SB if t == 1 else 0

    own_copies = []
    for s in range(STEPS):
        for t, (src, bufs) in enumerate(((k_hbm, kbufs), (v_hbm, vbufs))):
            for b in range(SB):
                cp = pltpu.make_async_copy(
                    src.at[s, pl.ds(b * BLK, BLK), cols], bufs[s].at[base(s, t) + SB * c + b], own_sem.at[s, t, b]
                )
                cp.start()
                own_copies.append((s, cp))
    q_copy = pltpu.make_async_copy(q_hbm, q_ref, load_sem)
    q_copy.start()

    def w_copy(n):
        return pltpu.make_async_copy(
            w_hbm.at[:, pl.ds(pl.multiple_of(n * NW, NW), NW)], w_ref.at[n], w_sem.at[n]
        )

    for n in range(NC):
        w_copy(n).start()

    barrier = pltpu.get_barrier_semaphore()
    pl.semaphore_signal(barrier, inc=1, device_id={"head": sib}, device_id_type=MESH)

    @pl.when(z > 0)
    def _():
        pl.semaphore_signal(barrier, inc=1, device_id={"head": h - 2}, device_id_type=MESH)

    @pl.when(z < Z - 1)
    def _():
        pl.semaphore_signal(barrier, inc=1, device_id={"head": h + 2}, device_id_type=MESH)

    for p in range(1, C):
        pl.semaphore_signal(barrier, inc=1, device_id={"ctx": lax.rem(c + p, C)}, device_id_type=MESH)
    pl.semaphore_wait(barrier, C + (z > 0).astype(jnp.int32) + (z < Z - 1).astype(jnp.int32))

    def kv_copy(s, t, p):
        src = (k_hbm, v_hbm)[t]
        buf = (kbufs, vbufs)[t][s]
        return pltpu.make_async_remote_copy(
            src_ref=src.at[s, own_rows, cols],
            dst_ref=buf.at[base(s, t) + SB * c + j],
            send_sem=kv_send.at[s, t, p],
            recv_sem=kv_recv.at[s, t, c],
            device_id={"ctx": lax.rem(c + p, C)},
            device_id_type=MESH,
        )

    def kv_arrival(s, t, origin, block, sem):
        buf = (kbufs, vbufs)[t][s]
        dst = buf.at[base(s, t) + SB * origin + block]
        return pltpu.make_async_copy(dst, dst, sem.at[s, t, origin])

    def fw_copy(s, t, p):
        origin = lax.rem(c + C - p, C)
        buf = (kbufs, vbufs)[t][s]
        return pltpu.make_async_remote_copy(
            src_ref=buf.at[base(s, t) + SB * origin + j],
            dst_ref=buf.at[base(s, t) + SB * origin + j],
            send_sem=fw_send.at[s, t, p],
            recv_sem=fw_recv.at[s, t, origin],
            device_id={"head": sib},
            device_id_type=MESH,
        )

    for s in range(STEPS):
        for p in range(1, C):
            for t in range(2):
                kv_copy(s, t, p).start()
    low = z < Z // 2
    zm = jnp.where(low, z, Z - 1 - z)

    def dest_of(t):
        paired = jnp.where(t % 2 == 0, Z - 1 - t // 2, t // 2)
        d = jnp.where(t < 2 * zm, paired, Z - 1 - (t - zm))
        return jnp.where(low, d, Z - 1 - d)

    d_first = dest_of(jnp.int32(0))
    b_first = (d_first * QR) // BLK

    def fill(s, b):
        place = jnp.int32(0)
        for p in range(C):
            place = jnp.where(owner[s, p] == c, p, place)
        block = (s * C + place) * SB + b

        def one_head(lh, carry):
            i = b * LH + lh
            head = h * LH + lh

            def put(tile, chosen, allowed):
                chosen = jnp.where(allowed, chosen, block)
                span = chosen // SB
                step = span // C
                holder = owner[step, span - step * C]
                tab_idx[s, i, tile] = (step * C + holder) * SB + chosen - span * SB
                tab_bias[s, i, tile] = jnp.where(allowed, 0.0, -1e30).astype(jnp.float32)

            vs = [vert[a, head] for a in range(NV)]
            put(0, block, block == block)
            for a in range(NV):
                put(1 + a, vs[a], vs[a] < block)
            for a in range(NS):
                row = block - slant[a, head]
                ok = row >= 0
                for x in vs:
                    ok = jnp.logical_and(ok, row != x)
                put(1 + NV + a, row, ok)
            return carry

        lax.fori_loop(0, LH, one_head, 0)

    for s in range(STEPS):
        fill(s, b_first)

    scale = math.log2(math.e) / math.sqrt(HD)

    row_ids = lax.broadcasted_iota(jnp.int32, (BLK, BLK), 0)
    col_ids = lax.broadcasted_iota(jnp.int32, (BLK, BLK), 1)

    def attend(b, s):
        rows = pl.ds(pl.multiple_of(b * BLK, BLK), BLK)

        def one(lh):
            hc = pl.ds(pl.multiple_of(lh * HD, HD), HD)
            i = b * LH + lh
            qt = q_ref[s, rows, hc]
            ids = [tab_idx[s, i, t] for t in range(NT)]

            kt = jnp.concatenate([kt_ref[ids[t]] for t in range(NT)], axis=1)
            sc = jnp.dot(qt, kt, preferred_element_type=jnp.float32)
            pieces = []
            for t in range(NT):
                x = sc[:, t * BLK:(t + 1) * BLK] * scale
                if t == 0:
                    x = jnp.where(col_ids <= row_ids, x, -1e30)
                else:
                    x = x + tab_bias[s, i, t]
                pieces.append(x)
            top = pieces[0]
            for x in pieces[1:]:
                top = jnp.maximum(top, x)
            top = jnp.max(top, axis=1, keepdims=True)
            ws = [jnp.exp2(x - top) for x in pieces]
            tot = ws[0]
            for x in ws[1:]:
                tot = tot + x
            tot = jnp.sum(tot, axis=1, keepdims=True)
            wt = jnp.concatenate([x.astype(jnp.bfloat16) for x in ws], axis=1)
            vt = jnp.concatenate([vbufs[s][ids[t]] for t in range(NT)], axis=0)
            mixed = jnp.dot(wt, vt, preferred_element_type=jnp.float32) * (1.0 / tot)
            att[s, rows, hc] = mixed.astype(jnp.bfloat16)

        def body(i, carry):
            one(2 * i)
            one(2 * i + 1)
            return carry

        lax.fori_loop(0, LH // 2, body, 0)

    def x_copy(d, n, s):
        return pltpu.make_async_remote_copy(
            src_ref=part.at[d, n, s, 1 - j], dst_ref=crecv.at[d, n, s],
            send_sem=x_send.at[d, n, s], recv_sem=x_recv.at[d, n, s],
            device_id={"head": sib}, device_id_type=MESH,
        )

    def u_copy(d, n, s):
        return pltpu.make_async_remote_copy(
            src_ref=part.at[d, n, s, j], dst_ref=urecv.at[d, n, s],
            send_sem=z_send.at[d, n, s], recv_sem=u_recv.at[d, n, s],
            device_id={"head": h + 2}, device_id_type=MESH,
        )

    def d_copy(d, n, s):
        return pltpu.make_async_remote_copy(
            src_ref=part.at[d, n, s, j], dst_ref=drecv.at[d, n, s],
            send_sem=z_send.at[d, n, s], recv_sem=d_recv.at[d, n, s],
            device_id={"head": h - 2}, device_id_type=MESH,
        )

    f32 = jnp.float32

    def process(d, n, s):
        x_copy(d, n, s).wait_recv()

        def ready(*more):
            total = part[d, n, s, j].astype(f32) + crecv[d, n, s].astype(f32)
            for buf in more:
                total = total + buf[d, n, s].astype(f32)
            part[d, n, s, j] = total.astype(jnp.bfloat16)

        @pl.when(d > z)
        def _():
            @pl.when(z > 0)
            def _():
                u_copy(d, n, s).wait_recv()
                ready(urecv)

            @pl.when(z == 0)
            def _():
                ready()

            u_copy(d, n, s).start()

        @pl.when(d < z)
        def _():
            @pl.when(z < Z - 1)
            def _():
                d_copy(d, n, s).wait_recv()
                ready(drecv)

            @pl.when(z == Z - 1)
            def _():
                ready()

            d_copy(d, n, s).start()

    at_end = jnp.logical_or(z == 0, z == Z - 1)

    def send_parts(d, n, y, ss):
        for i, s in enumerate(ss):
            for jj in range(2):
                part[d, n, s, jj] = y[(2 * i + jj) * RS:(2 * i + jj + 1) * RS]
            x_copy(d, n, s).start()

    def rows_of(d, s):
        return att[s, pl.ds(pl.multiple_of(d * QR, QR), QR), :]

    def project_first(d, s):
        def step(n, carry):
            if s == 0:
                w_copy(n).wait()
            y = jnp.dot(rows_of(d, s), w_ref[n], preferred_element_type=f32)
            send_parts(d, n, y.astype(jnp.bfloat16), (s,))

            @pl.when(jnp.logical_and(at_end, n > 0))
            def _():
                process(d, n - 1, s)

            return carry

        lax.fori_loop(0, NC, step, 0)

        @pl.when(at_end)
        def _():
            process(d, NC - 1, s)

    def project(t, d):
        prev = dest_of(t - 1)

        def step(n, carry):
            lhs = jnp.concatenate([rows_of(d, s) for s in range(STEPS)], axis=0)
            y = jnp.dot(lhs, w_ref[n], preferred_element_type=f32)
            send_parts(d, n, y.astype(jnp.bfloat16), range(STEPS))

            @pl.when(jnp.logical_and(at_end, jnp.logical_and(n > 0, d != z)))
            def _():
                for s in range(STEPS):
                    process(d, n - 1, s)

            @pl.when(jnp.logical_not(at_end))
            def _():
                for s in range(STEPS):
                    process(prev, n, s)

            return carry

        lax.fori_loop(0, NC, step, 0)

        @pl.when(jnp.logical_and(at_end, d != z))
        def _():
            for s in range(STEPS):
                process(d, NC - 1, s)

    early = [
        pltpu.make_async_copy(v0, v1.at[pl.ds(0, C * SB)], early_sem)
    ]
    q_copy.wait()
    for s in range(STEPS):
        for p in range(1, C):
            origin = lax.rem(c + C - p, C)
            for t in range(2):
                kv_arrival(s, t, origin, j, kv_recv).wait()
                fw_copy(s, t, p).start()
        for step_of, cp in own_copies:
            if step_of == s:
                cp.wait()
        for p in range(1, C):
            origin = lax.rem(c + C - p, C)
            for t in range(2):
                kv_arrival(s, t, origin, 1 - j, fw_recv).wait()
        def turn(i, carry, s=s):
            kt_ref[s * C * SB + i] = kbufs[s][i].T
            return carry

        lax.fori_loop(0, C * SB, turn, 0)
        if s == 0:
            for cp in early:
                cp.start()
        else:
            for cp in early:
                cp.wait()
        attend(b_first, s)
        project_first(d_first, s)
    for k in range(1, SB):
        for s in range(STEPS):
            fill(s, lax.rem(b_first + k, SB))

    def rest(t, carry):
        d = dest_of(t)
        b = (d * QR) // BLK
        fresh = t > 0
        for before in range(Z):
            other = (dest_of(jnp.int32(before)) * QR) // BLK
            fresh = jnp.logical_and(fresh, jnp.logical_or(before >= t, other != b))

        @pl.when(fresh)
        def _():
            for s in range(STEPS):
                attend(b, s)

        project(t, d)
        return carry

    lax.fori_loop(1, Z, rest, 0)

    def o_copy(n, s):
        return pltpu.make_async_copy(
            obuf.at[n, s],
            out_hbm.at[s, :, pl.ds(pl.multiple_of(n * NW, NW), NW)],
            o_sem.at[n, s],
        )

    def finish(n, carry):
        for s in range(STEPS):
            def done(*more, s=s):
                total = part[z, n, s, j].astype(f32) + crecv[z, n, s].astype(f32)
                for buf in more:
                    total = total + buf[z, n, s].astype(f32)
                obuf[n, s] = total.astype(jnp.bfloat16)

            x_copy(z, n, s).wait_recv()

            @pl.when(z == 0)
            def _():
                d_copy(z, n, s).wait_recv()
                done(drecv)

            @pl.when(z == Z - 1)
            def _():
                u_copy(z, n, s).wait_recv()
                done(urecv)

            @pl.when(jnp.logical_not(at_end))
            def _():
                d_copy(z, n, s).wait_recv()
                u_copy(z, n, s).wait_recv()
                done(drecv, urecv)

            o_copy(n, s).start()
        return carry

    def drain_z(i, carry):
        d = i // NC
        n = i % NC

        @pl.when(d > z)
        def _():
            for s in range(STEPS):
                u_copy(d, n, s).wait_send()

        @pl.when(d < z)
        def _():
            for s in range(STEPS):
                d_copy(d, n, s).wait_send()

        return carry

    def drain_x(i, carry):
        for s in range(STEPS):
            x_copy(i // NC, i % NC, s).wait_send()
        return carry

    for s in range(STEPS):
        for p in range(1, C):
            for t in range(2):
                kv_copy(s, t, p).wait_send()
                fw_copy(s, t, p).wait_send()
    lax.fori_loop(0, Z * NC, drain_x, 0)

    @pl.when(jnp.logical_not(at_end))
    def _():
        lax.fori_loop(0, Z * NC, drain_z, 0)

    lax.fori_loop(0, NC, finish, 0)

    @pl.when(at_end)
    def _():
        lax.fori_loop(0, Z * NC, drain_z, 0)

    def drain_out(n, carry):
        for s in range(STEPS):
            o_copy(n, s).wait()
        return carry

    lax.fori_loop(0, NC, drain_out, 0)


def solution(mesh):
    C = mesh.shape["ctx"]
    H = mesh.shape["head"]
    Z = H // 2

    def local(queries, key_rows, value_rows, out_weight, span_owner, vertical_blocks, slash_offsets):
        steps, span_rows, width = queries.shape
        depth, DW = out_weight.shape
        LH = width // HD
        RS = span_rows // H
        SB = span_rows // BLK
        NC = DW // NW
        NV, NS = vertical_blocks.shape[1], slash_offsets.shape[1]
        NT = 1 + NV + NS
        bf = jnp.bfloat16
        kv0 = pltpu.VMEM((C * SB, BLK, HD), bf)
        kt = pltpu.VMEM((STEPS * C * SB, HD, BLK), bf)
        kv1 = pltpu.VMEM((STEPS * C * SB, BLK, HD), bf)
        dma = pltpu.SemaphoreType.DMA
        smem = pl.BlockSpec(memory_space=pltpu.SMEM)
        anyspec = pl.BlockSpec(memory_space=pl.ANY)
        return pl.pallas_call(
            functools.partial(kernel, C, H, LH, RS, NV, NS),
            out_shape=jax.ShapeDtypeStruct((STEPS, RS, DW), bf),
            in_specs=[smem] * 3 + [anyspec] * 4,
            out_specs=anyspec,
            scratch_shapes=[
                pltpu.VMEM((STEPS, span_rows, width), bf),
                kv0, kv0, kv0, kv1, kt,
                pltpu.VMEM((NC, depth, NW), bf),
                pltpu.VMEM((STEPS, span_rows, width), bf),
                pltpu.VMEM((Z, NC, STEPS, 2, RS, NW), bf),
                pltpu.VMEM((Z, NC, STEPS, RS, NW), bf),
                pltpu.VMEM((Z, NC, STEPS, RS, NW), bf),
                pltpu.VMEM((Z, NC, STEPS, RS, NW), bf),
                pltpu.VMEM((NC, STEPS, RS, NW), bf),
                pltpu.SMEM((STEPS, SB * LH, NT), jnp.int32),
                pltpu.SMEM((STEPS, SB * LH, NT), jnp.float32),
                dma, dma((NC,)), dma((STEPS, 2, SB)),
                dma((STEPS, 2, C)), dma((STEPS, 2, C)), dma((STEPS, 2, C)), dma((STEPS, 2, C)),
                *[dma((Z, NC, STEPS))] * 5,
                dma((NC, STEPS)), dma,
            ],
            compiler_params=pltpu.CompilerParams(
                collective_id=0, has_side_effects=True, vmem_limit_bytes=58 * 1024 * 1024
            ),
            cost_estimate=pl.CostEstimate(
                flops=2 * STEPS * span_rows * depth * DW, bytes_accessed=depth * DW * 2, transcendentals=0
            ),
        )(span_owner, vertical_blocks.T, slash_offsets.T, queries, key_rows, value_rows, out_weight)

    in_specs = (
        P(None, "ctx", "head"),
        P(None, "ctx", None),
        P(None, "ctx", None),
        P("head", None),
        P(),
        P(),
        P(),
    )
    return jax.shard_map(
        local, mesh=mesh, in_specs=in_specs, out_specs=P(None, ("ctx", "head"), None), check_vma=False
    )
```
